512 devices in a mesh: row: 16 (over z_lo, x), col: 32 (over z_hi, y, core).
Axes of the slice: x: 4, y: 4, z: 16 (z_hi: 4, z_lo: 4; z = z_hi * 4 + z_lo), core: 2. Of those that a mesh axis runs over, the one named last changes fastest.
Arguments:
- inputs: bfloat16 [512, 12288], P('col', 'row'), may hold values from -6 to 6
- w_in: bfloat16 [12288, 24576], P('row', 'col'), may hold values from -0.0546875 to 0.0546875
- w_out: bfloat16 [24576, 12288], P('col', 'row'), may hold values from -0.0390625 to 0.0390625
- cotangent: bfloat16 [512, 12288], P('col', 'row'), may hold values from -6 to 6
Outputs:
- output: bfloat16 [512, 12288], P('col', 'row')
- grad_inputs: bfloat16 [512, 12288], P('col', 'row')
- grad_w_in: bfloat16 [12288, 24576], P('row', 'col')
- grad_w_out: bfloat16 [24576, 12288], P('col', 'row')
The draws below stay inside these ranges and needn't reach their ends.
All inputs are finite; a program needn't handle non-finite values.
Results may differ from the reference program's by a relative error of at most 0.034.
Values may be sent and summed in bfloat16 or wider, within the bound.
No kernel may reach another device: no remote copies, remote signals or barrier semaphores. Data moves between devices by JAX's collectives and lax.ppermute only.
A program may use at most 64 MiB of HBM per device.

```python
import jax
import jax.numpy as jnp
from jax import lax

D = 12288
FF = 24576
TOKENS = 512
N_ROW = 16
N_COL = 32


def shard_levels(own_key, dims, split, smallest, top_value):
    gain = 1.0
    for axis_at, blocks in split:
        heights = jax.random.uniform(jax.random.fold_in(jax.random.fold_in(own_key, 6), axis_at), (blocks,), jnp.float32, smallest / len(split), top_value / len(split))
        gain = gain * jnp.repeat(jnp.exp(heights), dims[axis_at] // blocks).reshape((-1,) + (1,) * (len(dims) - 1 - axis_at))
    return gain


def centred(key, extent, scale, bound, split=(), held_as=jnp.bfloat16):
    result = scale * jax.random.normal(key, extent, jnp.float32)
    if split:
        result = result * shard_levels(key, extent, split, -0.22, 0.18)
    return jnp.clip(result, -bound, bound).astype(held_as)


def setup_inputs(seed: int = 0) -> dict:
    arg_keys = jax.random.split(jax.random.key(seed), 5)
    return {
        "inputs": centred(arg_keys[0], (TOKENS, D), 1.0, 6.0, ((0, 32), (1, 16))),
        "w_in": centred(arg_keys[1], (D, FF), D ** -0.5, 0.0546875, ((0, 16), (1, 32))),
        "w_out": centred(arg_keys[2], (FF, D), FF ** -0.5, 0.0390625, ((0, 32), (1, 16))),
        "cotangent": centred(arg_keys[3], (TOKENS, D), 1.0, 6.0, ((0, 32), (1, 16))),
    }


def gelu_tanh(values):
    return jax.nn.gelu(values, approximate=True)

def gelu_grad(hidden, upstream):
    pullback = jax.vjp(gelu_tanh, hidden)[1]
    return pullback(upstream)[0]

def rounded(values):
    return lax.optimization_barrier(values.astype(jnp.bfloat16)).astype(jnp.float32)

def block_sum(make_term, number, shape):

    def advance(index, running):
        return running + rounded(make_term(index.astype(jnp.int32)))
    return lax.fori_loop(0, number, advance, jnp.zeros(shape, jnp.float32))

def reference(inputs, w_in, w_out, cotangent):
    width_block = D // N_ROW
    unit_block = FF // N_COL
    tokens = inputs.shape[0]

    def hidden_term(index):
        left = lax.dynamic_slice_in_dim(inputs, index * width_block, width_block, 1)
        right = lax.dynamic_slice_in_dim(w_in, index * width_block, width_block, 0)
        return jnp.dot(left, right, preferred_element_type=jnp.float32)
    hidden = block_sum(hidden_term, N_ROW, (tokens, FF))
    active = gelu_tanh(hidden).astype(jnp.bfloat16)

    def output_term(index):
        left = lax.dynamic_slice_in_dim(active, index * unit_block, unit_block, 1)
        right = lax.dynamic_slice_in_dim(w_out, index * unit_block, unit_block, 0)
        return jnp.dot(left, right, preferred_element_type=jnp.float32)
    output = block_sum(output_term, N_COL, (tokens, D)).astype(jnp.bfloat16)

    def active_term(index):
        left = lax.dynamic_slice_in_dim(cotangent, index * width_block, width_block, 1)
        right = lax.dynamic_slice_in_dim(w_out, index * width_block, width_block, 1)
        return lax.dot_general(left, right, (((1,), (1,)), ((), ())), preferred_element_type=jnp.float32)
    grad_active = block_sum(active_term, N_ROW, (tokens, FF))
    grad_hidden = gelu_grad(hidden, grad_active).astype(jnp.bfloat16)

    def input_term(index):
        left = lax.dynamic_slice_in_dim(grad_hidden, index * unit_block, unit_block, 1)
        right = lax.dynamic_slice_in_dim(w_in, index * unit_block, unit_block, 1)
        return lax.dot_general(left, right, (((1,), (1,)), ((), ())), preferred_element_type=jnp.float32)
    grad_inputs = block_sum(input_term, N_COL, (tokens, D)).astype(jnp.bfloat16)
    grad_w_in = lax.dot_general(inputs, grad_hidden, (((0,), (0,)), ((), ())), preferred_element_type=jnp.float32).astype(jnp.bfloat16)
    grad_w_out = lax.dot_general(active, cotangent, (((0,), (0,)), ((), ())), preferred_element_type=jnp.float32).astype(jnp.bfloat16)
    return (output, grad_inputs, grad_w_in, grad_w_out)
```

```python
import jax
import jax.numpy as jnp
from jax import lax
from jax.sharding import Mesh, PartitionSpec as P

F32 = jnp.float32
BF16 = jnp.bfloat16


def gelu_tanh(values):
    return jax.nn.gelu(values, approximate=True)


def product(left, right, dims):
    return lax.dot_general(left, right, (dims, ((), ())), preferred_element_type=F32).astype(BF16)


def exchange(parts, axis):
    return lax.all_to_all(parts, axis, 0, 0)


def gather(share, axis, size):
    return exchange(jnp.broadcast_to(share[None], (size, *share.shape)), axis)


def summed(parts):
    return jnp.sum(parts.astype(F32), axis=0)


def swap_cores(values):
    return lax.ppermute(values, "core", [(0, 1), (1, 0)])


def per_device(inputs, w_in, w_out, cotangent):
    rows, width = inputs.shape
    units = w_in.shape[1]
    size = {name: lax.axis_size(name) for name in ("z_lo", "x", "z_hi", "y", "core")}

    share = jnp.concatenate([inputs, cotangent], axis=1)
    own = gather(gather(share, "z_hi", size["z_hi"]), "y", size["y"])
    own = own.reshape(-1, 2 * width)
    other = swap_cores(own)
    half = own.shape[0]
    tokens = jnp.concatenate([own, other], axis=0)
    input_all, cotangent_all = tokens[:, :width], tokens[:, width:]

    terms = jnp.concatenate(
        [product(input_all, w_in, ((1,), (0,))), product(cotangent_all, w_out, ((1,), (1,)))], axis=1
    )
    parts = exchange(terms.reshape(size["x"], -1, 2 * units), "x")
    parts = summed(parts).astype(BF16).reshape(size["z_lo"], -1, 2 * units)
    both = summed(exchange(parts, "z_lo"))
    hidden, grad_active = both[:, :units], both[:, units:]
    active, pullback = jax.vjp(gelu_tanh, hidden)
    share = jnp.concatenate([active.astype(BF16), pullback(grad_active)[0].astype(BF16)], axis=1)
    both = gather(gather(share, "z_lo", size["z_lo"]), "x", size["x"]).reshape(2 * half, 2 * units)
    active_all, grad_hidden_all = both[:, :units], both[:, units:]

    def layer_terms(rows):
        return jnp.concatenate(
            [
                product(active_all[rows], w_out, ((1,), (0,))),
                product(grad_hidden_all[rows], w_in, ((1,), (1,))),
            ],
            axis=1,
        )

    arriving = swap_cores(layer_terms(slice(half, None)))
    kept = layer_terms(slice(0, half))
    grad_w_in = product(input_all, grad_hidden_all, ((0,), (0,)))
    grad_w_out = product(active_all, cotangent_all, ((0,), (0,)))
    parts = (kept.astype(F32) + arriving.astype(F32)).astype(BF16)
    parts = exchange(parts.reshape(size["y"], -1, 2 * width), "y")
    parts = summed(parts).astype(BF16).reshape(size["z_hi"], -1, 2 * width)
    both = summed(exchange(parts, "z_hi")).astype(BF16)
    return both[:, :width], both[:, width:], grad_w_in, grad_w_out


def solution(mesh):
    fine = Mesh(mesh.devices.reshape(4, 4, 4, 4, 2), ("z_lo", "x", "z_hi", "y", "core"))
    row, col = ("z_lo", "x"), ("z_hi", "y", "core")
    return jax.shard_map(
        per_device,
        mesh=fine,
        in_specs=(P(col, row), P(row, col), P(col, row), P(col, row)),
        out_specs=(P(col, row), P(col, row), P(row, col), P(col, row)),
        check_vma=False,
    )
```

```python
import jax
import jax.numpy as jnp
from jax import lax
from jax.sharding import Mesh, PartitionSpec as P

F32 = jnp.float32
BF16 = jnp.bfloat16


def gelu_tanh(values):
    return jax.nn.gelu(values, approximate=True)


def product(left, right, dims):
    return lax.dot_general(left, right, (dims, ((), ())), preferred_element_type=F32).astype(BF16)


def exchange(parts, axis):
    return lax.all_to_all(parts, axis, 0, 0)


def gather(share, axis, size):
    return exchange(jnp.broadcast_to(share[None], (size, *share.shape)), axis)


def summed(parts):
    return jnp.sum(parts.astype(F32), axis=0)


def swapped(values, axis):
    return lax.ppermute(values, axis, [(0, 1), (1, 0)])


def per_device(inputs, w_in, w_out, cotangent):
    rows, width = inputs.shape
    units = w_in.shape[1]
    size = {name: lax.axis_size(name) for name in ("z_pair", "x", "z_hi", "y")}
    plane = size["z_pair"] * size["x"]

    share = jnp.concatenate([inputs, cotangent], axis=1)
    own = gather(gather(share, "z_hi", size["z_hi"]), "y", size["y"])
    own = own.reshape(-1, 2 * width)
    other = swapped(own, "core")
    half = own.shape[0]
    tokens = jnp.concatenate([own, other], axis=0)
    input_all, cotangent_all = tokens[:, :width], tokens[:, width:]

    terms = jnp.concatenate(
        [product(input_all, w_in, ((1,), (0,))), product(cotangent_all, w_out, ((1,), (1,)))], axis=1
    )
    parts = exchange(terms.reshape(plane, -1, 2 * units), ("z_pair", "x"))
    part = summed(parts).astype(BF16)
    both = part.astype(F32) + swapped(part, "z_half").astype(F32)
    hidden, grad_active = both[:, :units], both[:, units:]
    active, pullback = jax.vjp(gelu_tanh, hidden)
    share = jnp.concatenate([active.astype(BF16), pullback(grad_active)[0].astype(BF16)], axis=1)
    both = gather(share, ("z_pair", "x"), plane).reshape(2 * half, 2 * units)
    active_all, grad_hidden_all = both[:, :units], both[:, units:]

    def layer_terms(rows):
        return jnp.concatenate(
            [
                product(active_all[rows], w_out, ((1,), (0,))),
                product(grad_hidden_all[rows], w_in, ((1,), (1,))),
            ],
            axis=1,
        )

    arriving = swapped(layer_terms(slice(half, None)), "core")
    kept = layer_terms(slice(0, half))
    grad_w_in = product(input_all, grad_hidden_all, ((0,), (0,)))
    grad_w_out = product(active_all, cotangent_all, ((0,), (0,)))
    parts = (kept.astype(F32) + arriving.astype(F32)).astype(BF16)
    parts = exchange(parts.reshape(size["y"], -1, 2 * width), "y")
    parts = summed(parts).astype(BF16).reshape(size["z_hi"], -1, 2 * width)
    both = summed(exchange(parts, "z_hi")).astype(BF16)
    return both[:, :width], both[:, width:], grad_w_in, grad_w_out


def solution(mesh):
    names = ("z_half", "z_pair", "x", "z_hi", "y", "core")
    fine = Mesh(mesh.devices.reshape(2, 2, 4, 4, 4, 2), names)
    row, col = names[:3], names[3:]
    return jax.shard_map(
        per_device,
        mesh=fine,
        in_specs=(P(col, row), P(row, col), P(col, row), P(col, row)),
        out_specs=(P(col, row), P(col, row), P(row, col), P(col, row)),
        check_vma=False,
    )
```

```python
import jax
import jax.numpy as jnp
from jax import lax
from jax.sharding import Mesh, PartitionSpec as P

F32 = jnp.float32
BF16 = jnp.bfloat16


def gelu_tanh(values):
    return jax.nn.gelu(values, approximate=True)


def product(left, right, dims):
    return lax.dot_general(left, right, (dims, ((), ())), preferred_element_type=F32).astype(BF16)


def exchange(parts, axis):
    return lax.all_to_all(parts, axis, 0, 0)


def gather(share, axis, size):
    return exchange(jnp.broadcast_to(share[None], (size, *share.shape)), axis)


def summed(parts):
    return jnp.sum(parts.astype(F32), axis=0)


def swapped(values, axis):
    return lax.ppermute(values, axis, [(0, 1), (1, 0)])


def together(*values):
    return lax.optimization_barrier(values)


def per_device(inputs, w_in, w_out, cotangent):
    rows, width = inputs.shape
    units = w_in.shape[1]
    size = {name: lax.axis_size(name) for name in ("z_pair", "x", "z_hi", "y")}
    plane = size["z_pair"] * size["x"]

    def hidden_terms(tokens):
        terms = [
            product(tokens[:, :width], w_in, ((1,), (0,))),
            product(tokens[:, width:], w_out, ((1,), (1,))),
        ]
        return jnp.concatenate(terms, axis=1).reshape(plane, -1, 2 * units)

    def layer_terms(both):
        terms = [
            product(both[:, :units], w_out, ((1,), (0,))),
            product(both[:, units:], w_in, ((1,), (1,))),
        ]
        return jnp.concatenate(terms, axis=1)

    def row_part(terms):
        return summed(exchange(terms, ("z_pair", "x"))).astype(BF16)

    def copies(part):
        both = part.astype(F32) + swapped(part, "z_half").astype(F32)
        active, pullback = jax.vjp(gelu_tanh, both[:, :units])
        share = jnp.concatenate([active.astype(BF16), pullback(both[:, units:])[0].astype(BF16)], axis=1)
        return jnp.broadcast_to(share[None], (plane, *share.shape))

    share = jnp.concatenate([inputs, cotangent], axis=1)
    own = gather(gather(share, "z_hi", size["z_hi"]), "y", size["y"]).reshape(-1, 2 * width)
    other = swapped(own, "core")
    own_terms, terms = together(hidden_terms(own), hidden_terms(other))
    other_part = row_part(terms)
    own_part = row_part(own_terms)
    share, own_part = together(copies(other_part), own_part)
    other_both = exchange(share, ("z_pair", "x"))
    share, other_both = together(copies(own_part), other_both)
    own_both = exchange(share, ("z_pair", "x")).reshape(-1, 2 * units)
    other_both = other_both.reshape(-1, 2 * units)

    kept = layer_terms(own_both)
    arriving = swapped(layer_terms(other_both), "core")
    parts = (kept.astype(F32) + arriving.astype(F32)).astype(BF16)
    parts = exchange(parts.reshape(size["y"], -1, 2 * width), "y")
    parts = summed(parts).astype(BF16).reshape(size["z_hi"], -1, 2 * width)
    output = summed(exchange(parts, "z_hi")).astype(BF16)

    tokens = jnp.concatenate([own, other], axis=0)
    both = jnp.concatenate([own_both, other_both], axis=0)
    grad_w_in = product(tokens[:, :width], both[:, units:], ((0,), (0,)))
    grad_w_out = product(both[:, :units], tokens[:, width:], ((0,), (0,)))
    return output[:, :width], output[:, width:], grad_w_in, grad_w_out


def solution(mesh):
    names = ("z_half", "z_pair", "x", "z_hi", "y", "core")
    fine = Mesh(mesh.devices.reshape(2, 2, 4, 4, 4, 2), names)
    row, col = names[:3], names[3:]
    return jax.shard_map(
        per_device,
        mesh=fine,
        in_specs=(P(col, row), P(row, col), P(col, row), P(col, row)),
        out_specs=(P(col, row), P(col, row), P(row, col), P(col, row)),
        check_vma=False,
    )
```

```python
import jax
import jax.numpy as jnp
from jax import lax
from jax.sharding import Mesh, PartitionSpec as P

F32 = jnp.float32
BF16 = jnp.bfloat16


def gelu_tanh(values):
    return jax.nn.gelu(values, approximate=True)


def product(left, right, dims):
    return lax.dot_general(left, right, (dims, ((), ())), preferred_element_type=F32).astype(BF16)


def exchange(parts, axis):
    return lax.all_to_all(parts, axis, 0, 0)


def gather(share, axis, size):
    return exchange(jnp.broadcast_to(share[None], (size, *share.shape)), axis)


def summed(parts):
    return jnp.sum(parts.astype(F32), axis=0)


def swapped(values, axis):
    return lax.ppermute(values, axis, [(0, 1), (1, 0)])


def together(*values):
    return lax.optimization_barrier(values)


def per_device(inputs, w_in, w_out, cotangent):
    rows, width = inputs.shape
    units = w_in.shape[1]
    size = {name: lax.axis_size(name) for name in ("z_pair", "x", "z_hi", "y")}
    plane = size["z_pair"] * size["x"]

    def hidden_terms(tokens):
        terms = [
            product(tokens[:, :width], w_in, ((1,), (0,))),
            product(tokens[:, width:], w_out, ((1,), (1,))),
        ]
        return jnp.concatenate(terms, axis=1).reshape(plane, -1, 2 * units)

    def layer_terms(both):
        return (
            lax.dot_general(both[:, :units], w_out, (((1,), (0,)), ((), ())), preferred_element_type=F32),
            lax.dot_general(both[:, units:], w_in, (((1,), (1,)), ((), ())), preferred_element_type=F32),
        )

    def row_part(terms):
        return summed(exchange(terms, ("z_pair", "x"))).astype(BF16)

    def copies(part):
        both = part.astype(F32) + swapped(part, "z_half").astype(F32)
        active, pullback = jax.vjp(gelu_tanh, both[:, :units])
        share = jnp.concatenate([active.astype(BF16), pullback(both[:, units:])[0].astype(BF16)], axis=1)
        return jnp.broadcast_to(share[None], (plane, *share.shape))

    share = jnp.concatenate([inputs, cotangent], axis=1)
    own = gather(gather(share, "z_hi", size["z_hi"]), "y", size["y"]).reshape(-1, 2 * width)
    other = swapped(own, "core")
    own_terms, terms = together(hidden_terms(own), hidden_terms(other))
    other_part = row_part(terms)
    own_part = row_part(own_terms)
    share, own_part = together(copies(other_part), own_part)
    other_both = exchange(share, ("z_pair", "x"))
    share, other_both = together(copies(own_part), other_both)
    own_both = exchange(share, ("z_pair", "x")).reshape(-1, 2 * units)
    other_both = other_both.reshape(-1, 2 * units)

    arriving = swapped(jnp.concatenate([term.astype(BF16) for term in layer_terms(other_both)], axis=1), "core")
    arriving = [arriving[:, :width], arriving[:, width:]]
    parts = [(kept + term.astype(F32)).astype(BF16) for kept, term in zip(layer_terms(own_both), arriving)]
    parts = jnp.concatenate(parts, axis=1)
    parts = exchange(parts.reshape(size["y"], -1, 2 * width), "y")
    parts = summed(parts).astype(BF16).reshape(size["z_hi"], -1, 2 * width)
    output = summed(exchange(parts, "z_hi")).astype(BF16)

    tokens = jnp.concatenate([own, other], axis=0)
    both = jnp.concatenate([own_both, other_both], axis=0)
    grad_w_in = product(tokens[:, :width], both[:, units:], ((0,), (0,)))
    grad_w_out = product(both[:, :units], tokens[:, width:], ((0,), (0,)))
    return output[:, :width], output[:, width:], grad_w_in, grad_w_out


def solution(mesh):
    names = ("z_half", "z_pair", "x", "z_hi", "y", "core")
    fine = Mesh(mesh.devices.reshape(2, 2, 4, 4, 4, 2), names)
    row, col = names[:3], names[3:]
    return jax.shard_map(
        per_device,
        mesh=fine,
        in_specs=(P(col, row), P(row, col), P(col, row), P(col, row)),
        out_specs=(P(col, row), P(col, row), P(row, col), P(col, row)),
        check_vma=False,
    )
```
